256 devices in a mesh: dp: 64 (over x, z, y_hi), mp: 4 (over y_lo, core).
Axes of the slice: x: 4, y: 4 (y_hi: 2, y_lo: 2; y = y_hi * 2 + y_lo), z: 8, core: 2. Of those that a mesh axis runs over, the one named last changes fastest.
Arguments:
- inputs: bfloat16 [8192, 4096], P('dp', 'mp'), may hold values from -6 to 6
- upstream: bfloat16 [8192, 4096], P('dp', 'mp'), may hold values from -6 to 6
- width_operator: bfloat16 [2560, 4096], P('dp', 'mp'), may hold values from -0.09375 to 0.09375
- query_weight: bfloat16 [2560, 2560], P('dp', 'mp'), may hold values from -0.125 to 0.125
- output_weight: bfloat16 [2560, 2560], P('dp', 'mp'), may hold values from -0.125 to 0.125
Outputs:
- grown: bfloat16 [8192, 4096], P('dp', 'mp')
- operator_grad: float32 [2560, 4096], P('dp', 'mp')
The draws below stay inside these ranges and needn't reach their ends.
All inputs are finite; a program needn't handle non-finite values.
Results may differ from the reference program's by a relative error of at most 0.012.
Values may be sent and summed in bfloat16 or wider, within the bound.
No kernel may reach another device: no remote copies, remote signals or barrier semaphores. Data moves between devices by JAX's collectives and lax.ppermute only.
A program may use at most 64 MiB of HBM per device.

```python
import math
import jax
import jax.numpy as jnp

S = 2560
GW = 4096
TOKENS = 8192


def levels(stream_key, dims, cuts, smallest, top_value):
    loudness, own = 1.0, jax.random.fold_in(stream_key, 6)
    for axis_at, blocks in cuts:
        heights = jnp.exp(jax.random.uniform(jax.random.fold_in(own, axis_at), (blocks,), jnp.float32, smallest / len(cuts), top_value / len(cuts)))
        loudness = loudness * jnp.repeat(heights, dims[axis_at] // blocks).reshape([-1 if axis == axis_at else 1 for axis in range(len(dims))])
    return loudness


def gaussian(rng, extent, spread, most, split=(), held_as=jnp.bfloat16):
    gain = levels(rng, extent, split, -0.22, 0.18) if split else 1.0
    result = jax.random.normal(rng, extent, jnp.float32) * spread * gain
    return jnp.minimum(jnp.maximum(result, -most), most).astype(held_as)


def setup_inputs(seed: int = 0) -> dict:
    arg_keys = jax.random.split(jax.random.key(seed), 6)
    return {
        "inputs": gaussian(arg_keys[0], (TOKENS, GW), 1.0, 6.0, ((0, 64), (1, 4))),
        "upstream": gaussian(arg_keys[1], (TOKENS, GW), 1.0, 6.0, ((0, 64), (1, 4))),
        "width_operator": gaussian(arg_keys[2], (S, GW), GW ** -0.5, 0.09375, ((0, 64), (1, 4))),
        "query_weight": gaussian(arg_keys[3], (S, S), S ** -0.5, 0.125, ((0, 64), (1, 4))),
        "output_weight": gaussian(arg_keys[4], (S, S), S ** -0.5, 0.125, ((0, 64), (1, 4))),
    }


def reference(inputs, upstream, width_operator, query_weight, output_weight):
    operator = width_operator

    def reduce_features(values):
        return jnp.dot(values, operator.T, preferred_element_type=jnp.float32).astype(jnp.bfloat16)

    def expand_features(values):
        return jnp.dot(values, operator, preferred_element_type=jnp.float32).astype(jnp.bfloat16)

    def project(values, weight):
        return jnp.dot(values, weight, preferred_element_type=jnp.float32).astype(jnp.bfloat16)
    feat_low = reduce_features(inputs)
    query_low = project(feat_low, query_weight)
    grown_query = expand_features(query_low)
    back_low = reduce_features(grown_query)
    out_low = project(back_low, output_weight)
    grown = expand_features(out_low)
    cot_out_low = reduce_features(upstream)
    cot_back_low = project(cot_out_low, output_weight.T)
    cot_query = expand_features(cot_back_low)
    cot_query_low = reduce_features(cot_query)
    cot_feat_low = project(cot_query_low, query_weight.T)
    left_side = jnp.concatenate([out_low, cot_back_low, query_low, cot_feat_low], 0)
    right_side = jnp.concatenate([upstream, grown_query, cot_query, inputs], 0)
    operator_grad = jnp.dot(left_side.T, right_side, preferred_element_type=jnp.float32) / math.sqrt(TOKENS)
    return (grown, operator_grad)
```

```python
import math

import jax
import jax.numpy as jnp
from jax import lax
from jax.sharding import PartitionSpec as P

X, Z, Y = 4, 8, 2
BF = jnp.bfloat16
F32 = jnp.float32


def shift(value, dx=0, dz=0, dy=0):
    pairs = []
    for x in range(X):
        for z in range(Z):
            for y in range(Y):
                target = (((x + dx) % X) * Z + (z + dz) % Z) * Y + (y + dy) % Y
                pairs.append(((x * Z + z) * Y + y, target))
    return lax.ppermute(value, "dp", pairs)


def swap(value, bit):
    return lax.ppermute(value, "mp", [(i, i ^ bit) for i in range(4)])


def put(buffer, block, axis, index):
    starts = [0] * buffer.ndim
    starts[axis] = index
    return lax.dynamic_update_slice(buffer, jnp.expand_dims(block, axis), starts)


def ring_gather(block, axis_name, size, me, axis):
    shape = block.shape[:axis] + (size,) + block.shape[axis:]
    out = put(jnp.zeros(shape, block.dtype), block, axis, me)
    up = down = block
    for step in range(1, size // 2):
        up = shift(up, **{axis_name: 1})
        down = shift(down, **{axis_name: -1})
        out = put(out, up, axis, (me - step) % size)
        out = put(out, down, axis, (me + step) % size)
    half = block.shape[0] // 2
    up = shift(up[:half], **{axis_name: 1})
    down = shift(down[half:], **{axis_name: -1})
    return put(out, jnp.concatenate([up, down], 0), axis, (me + size // 2) % size)


def dot(a, b, dims):
    return lax.dot_general(a, b, (dims, ((), ())), preferred_element_type=F32)


def columns(value, index, width):
    return lax.dynamic_slice_in_dim(value, index * width, width, 1)


def mp_reduce(partial, y_lo, core):
    rows, width = partial.shape[0], partial.shape[1] // 4
    order = (y_lo * 2, 2 - y_lo * 2)
    send = jnp.concatenate([columns(partial, o + 1 - core, width) for o in order], 0)
    keep = jnp.concatenate([columns(partial, o + core, width) for o in order], 0)
    total = keep.astype(F32) + swap(send, 1).astype(F32)
    other = swap(total[rows:].astype(BF), 2)
    return (total[:rows] + other.astype(F32)).astype(BF)


def mp_gather(block, y_lo, core):
    rows = block.shape[0]
    pair = jnp.concatenate([block, swap(block, 2)], 0)
    beside = swap(pair, 1)
    even = jnp.where(core == 0, pair, beside)
    odd = jnp.where(core == 0, beside, pair)
    near, far = jnp.concatenate([even[:rows], odd[:rows]], 1), jnp.concatenate([even[rows:], odd[rows:]], 1)
    low = y_lo == 0
    return jnp.concatenate([jnp.where(low, near, far), jnp.where(low, far, near)], 1)


def add(*values):
    total = values[0].astype(F32)
    for v in values[1:]:
        total = total + v.astype(F32)
    return total


def direct_scatter(blocks, axis_name, size, me):
    def block(d):
        return lax.dynamic_index_in_dim(blocks, (me + d) % size, 0, keepdims=False)

    got = [shift(block(d), **{axis_name: d}) for d in range(1, size)]
    return add(block(0), *got)


def ring_scatter(blocks, axis_name, size, me):
    def block(d):
        return lax.dynamic_index_in_dim(blocks, (me + d) % size, 1, keepdims=False)

    far = size // 2
    half = blocks.shape[0] // 2
    up = shift(block(far)[:half], **{axis_name: 1})
    down = shift(block(far)[half:], **{axis_name: -1})
    for d in range(far - 1, 0, -1):
        a, b = block(d), block(-d)
        if d == far - 1:
            a = jnp.concatenate([add(a[:half], up).astype(BF), a[half:]], 0)
            b = jnp.concatenate([b[:half], add(b[half:], down).astype(BF)], 0)
        else:
            a, b = add(a, up).astype(BF), add(b, down).astype(BF)
        up, down = shift(a, **{axis_name: 1}), shift(b, **{axis_name: -1})
    return add(block(0), up, down)


def scatter_gradient(first, second, x, z, y):
    rows = first.shape[0] // (X * Z * Y)
    a = direct_scatter(first.reshape(X, Z * Y * rows, -1), "dx", X, x).astype(BF)
    b = ring_scatter(second.reshape(X, Z, Y * rows, -1), "dz", Z, z).astype(BF)
    b = direct_scatter(b, "dx", X, x)
    a = direct_scatter(a.reshape(Z, Y * rows, -1), "dz", Z, z)
    both = jnp.concatenate([a, b], 1).reshape(Y, rows, -1)
    send = lax.dynamic_index_in_dim(both, 1 - y, 0, keepdims=False).astype(BF)
    keep = lax.dynamic_index_in_dim(both, y, 0, keepdims=False)
    return keep + shift(send, dy=1).astype(F32)


def on_device(inputs, upstream, width_operator, query_weight, output_weight):
    dp, mp = lax.axis_index("dp"), lax.axis_index("mp")
    x, z, y = dp // (Z * Y), dp // Y % Z, dp % Y
    y_lo, core = mp // 2, mp % 2
    rows, features = width_operator.shape
    block = query_weight.shape[1]
    tokens = inputs.shape[0]

    mine = jnp.concatenate([width_operator, query_weight, output_weight], 1)
    other = shift(mine, dy=1)
    pair = jnp.where(y == 0, jnp.stack([mine, other]), jnp.stack([other, mine]))
    operator = ring_gather(pair[:, :, :features].reshape(Y * rows, features), "dx", X, x, 0)
    operator = ring_gather(operator, "dz", Z, z, 1).reshape(-1, features)
    weights = ring_gather(pair[:, :, features:].reshape(Y * rows, 2 * block), "dz", Z, z, 0)
    weights = ring_gather(weights, "dx", X, x, 0).reshape(-1, 2 * block)
    query_slab, output_slab = weights[:, :block], weights[:, block:]

    def contract(values):
        return mp_reduce(dot(values, operator, ((1,), (1,))).astype(BF), y_lo, core)

    def expand(values):
        return dot(values, operator, ((1,), (0,))).astype(BF)

    def project(low, slab, back, back_slab):
        whole = mp_gather(low, y_lo, core)
        back = mp_reduce(dot(back, back_slab, ((1,), (1,))).astype(BF), y_lo, core)
        low = dot(whole, slab, ((1,), (0,))).astype(BF)
        return mp_gather(jnp.concatenate([low, back], 0), y_lo, core)

    low = contract(jnp.concatenate([inputs, upstream], 0))
    query_and_back = project(low[:tokens], query_slab, low[tokens:], output_slab)
    grown_both = expand(query_and_back)
    low = contract(grown_both)
    out_and_feat = project(low[:tokens], output_slab, low[tokens:], query_slab)
    grown = expand(out_and_feat[:tokens])

    scale = 1.0 / math.sqrt(tokens * X * Z * Y)
    left = jnp.concatenate([out_and_feat, query_and_back[tokens:], query_and_back[:tokens]], 0)
    right = jnp.concatenate([upstream, inputs, grown_both], 0)
    half = features // 2
    first = (dot(left, right[:, :half], ((0,), (0,))) * scale).astype(BF)
    second = (dot(left, right[:, half:], ((0,), (0,))) * scale).astype(BF)
    return (grown, scatter_gradient(first, second, x, z, y))


def solution(mesh):
    return jax.shard_map(
        on_device,
        mesh=mesh,
        in_specs=(P("dp", "mp"), P("dp", "mp"), P("dp", "mp"), P("dp", "mp"), P("dp", "mp")),
        out_specs=(P("dp", "mp"), P("dp", "mp")),
        check_vma=False,
    )
```

```python
import functools
import math

import jax
import jax.numpy as jnp
from jax import lax
from jax.experimental import pallas as pl
from jax.experimental.pallas import tpu as pltpu
from jax.sharding import PartitionSpec as P

X, Z, Y = 4, 8, 2
BF = jnp.bfloat16
F32 = jnp.float32


def shift(value, dx=0, dz=0, dy=0):
    pairs = []
    for x in range(X):
        for z in range(Z):
            for y in range(Y):
                target = (((x + dx) % X) * Z + (z + dz) % Z) * Y + (y + dy) % Y
                pairs.append(((x * Z + z) * Y + y, target))
    return lax.ppermute(value, "dp", pairs)


def swap(value, bit):
    return lax.ppermute(value, "mp", [(i, i ^ bit) for i in range(4)])


def put(buffer, block, axis, index):
    starts = [0] * buffer.ndim
    starts[axis] = index
    return lax.dynamic_update_slice(buffer, jnp.expand_dims(block, axis), starts)


def ring_gather(block, axis_name, size, me, axis):
    shape = block.shape[:axis] + (size,) + block.shape[axis:]
    out = put(jnp.zeros(shape, block.dtype), block, axis, me)
    up = down = block
    for step in range(1, size // 2):
        up = shift(up, **{axis_name: 1})
        down = shift(down, **{axis_name: -1})
        out = put(out, up, axis, (me - step) % size)
        out = put(out, down, axis, (me + step) % size)
    half = block.shape[0] // 2
    up = shift(up[:half], **{axis_name: 1})
    down = shift(down[half:], **{axis_name: -1})
    return put(out, jnp.concatenate([up, down], 0), axis, (me + size // 2) % size)


def direct_gather(block, axis_name, size, me, axis):
    shape = block.shape[:axis] + (size,) + block.shape[axis:]
    order = sorted(range(1, size), key=lambda d: -min(d, size - d))
    got = {d: shift(block, **{axis_name: d}) for d in order}
    out = put(jnp.zeros(shape, block.dtype), block, axis, me)
    for d in order:
        out = put(out, got[d], axis, (me - d) % size)
    return out


def dot(a, b, dims):
    return lax.dot_general(a, b, (dims, ((), ())), preferred_element_type=F32)


def columns(value, index, width):
    return lax.dynamic_slice_in_dim(value, index * width, width, 1)


def mp_reduce(partial, y_lo, core):
    rows, width = partial.shape[0], partial.shape[1] // 4
    order = (y_lo * 2, 2 - y_lo * 2)
    send = jnp.concatenate([columns(partial, o + 1 - core, width) for o in order], 0)
    keep = jnp.concatenate([columns(partial, o + core, width) for o in order], 0)
    total = keep.astype(F32) + swap(send, 1).astype(F32)
    other = swap(total[rows:].astype(BF), 2)
    return (total[:rows] + other.astype(F32)).astype(BF)


def mp_blocks(block):
    far = swap(block, 2)
    return [block, swap(block, 1), far, swap(far, 1)]


def mp_gather(block, y_lo, core):
    own, beside, far, diagonal = mp_blocks(block)
    first, low = core == 0, y_lo == 0
    near = jnp.where(first, own, beside), jnp.where(first, beside, own)
    away = jnp.where(first, far, diagonal), jnp.where(first, diagonal, far)
    return jnp.concatenate([jnp.where(low, n, a) for n, a in zip(near, away)] + [jnp.where(low, a, n) for n, a in zip(near, away)], 1)


def add(*values):
    total = values[0].astype(F32)
    for v in values[1:]:
        total = total + v.astype(F32)
    return total


def first_kernel(scale, width, position, own, beside, far, diagonal, early, both, grown, ordered, *blocks):
    for flipped, rows in enumerate((own, beside, far, diagonal)):
        ordered[position[1] ^ flipped] = rows[...]
    right = jnp.concatenate([both[:, :width], grown[:, :width]], 0)
    for d, block in enumerate(blocks):
        owner = lax.rem(position[0] + d, len(blocks))
        left = jnp.concatenate([ordered[owner], early[owner]], 1)
        total = lax.dot_general(left, right, (((1,), (0,)), ((), ())), preferred_element_type=F32)
        block[...] = (total * scale).astype(BF)


def second_kernel(scale, width, position, late, early, both, grown, *blocks):
    right = jnp.concatenate([both[:, -width:], grown[:, -width:]], 0)
    outer, _, rows, tokens = late.shape
    for d, block in enumerate(blocks):
        owner = lax.rem(position[0] + d, len(blocks))
        left = [side[:, owner].reshape(outer * rows, tokens) for side in (late, early)]
        total = lax.dot_general(
            jnp.concatenate(left, 1), right, (((1,), (0,)), ((), ())), preferred_element_type=F32
        )
        block[...] = (total * scale).astype(BF).reshape(block.shape)


def call_product(kernel, position, operands, shapes, seconds):
    vmem = pl.BlockSpec(memory_space=pltpu.VMEM)
    return pl.pallas_call(
        kernel,
        out_shape=[jax.ShapeDtypeStruct(shape, BF) for shape in shapes],
        in_specs=[pl.BlockSpec(memory_space=pltpu.SMEM)] + [pl.BlockSpec(v.shape) for v in operands],
        out_specs=[vmem] * len(shapes),
        compiler_params=pltpu.CompilerParams(vmem_limit_bytes=40 << 20),
        cost_estimate=pl.CostEstimate(
            flops=int(seconds * 1e15), bytes_accessed=int(seconds * 3e12), transcendentals=0
        ),
    )(position, *operands)


def direct_scatter(blocks, axis_name):
    size = len(blocks)
    order = sorted(range(1, size), key=lambda d: -min(d, size - d))
    got = [shift(blocks[d], **{axis_name: d}) for d in order]
    return add(blocks[0], *got)


def ring_scatter(blocks, axis_name, beside):
    size = len(blocks)
    far = size // 2
    half = blocks[0].shape[0] // 2
    up = shift(blocks[far][:half], **{axis_name: 1})
    down = shift(blocks[far][half:], **{axis_name: -1})
    for d in range(far - 1, 0, -1):
        a, b = blocks[d], blocks[-d]
        if d == far - 1:
            a = jnp.concatenate([add(a[:half], up).astype(BF), a[half:]], 0)
            b = jnp.concatenate([b[:half], add(b[half:], down).astype(BF)], 0)
        else:
            a, b = add(a, up).astype(BF), add(b, down).astype(BF)
        if d == 1:
            a, b, beside = lax.optimization_barrier((a, b, beside))
        up, down = shift(a, **{axis_name: 1}), shift(b, **{axis_name: -1})
    return add(blocks[0], up, down), beside


def by_owner(value, size, me):
    return [lax.dynamic_index_in_dim(value, (me + d) % size, 0, keepdims=False) for d in range(size)]


def scatter_gradient(first, second, grown, x, z, y):
    a = direct_scatter(first, "dx").astype(BF)
    b, (a, grown) = ring_scatter(second, "dz", (a, grown))
    b = direct_scatter(by_owner(b.astype(BF), X, x), "dx")
    a = direct_scatter(by_owner(a.reshape(Z, -1, a.shape[-1]), Z, z), "dz")
    both = jnp.concatenate([a, b], 1)
    both = both.reshape(Y, -1, both.shape[-1])
    send = lax.dynamic_index_in_dim(both, 1 - y, 0, keepdims=False).astype(BF)
    keep = lax.dynamic_index_in_dim(both, y, 0, keepdims=False)
    return grown, keep + shift(send, dy=1).astype(F32)


def on_device(inputs, upstream, width_operator, query_weight, output_weight):
    dp, mp = lax.axis_index("dp"), lax.axis_index("mp")
    x, z, y = dp // (Z * Y), dp // Y % Z, dp % Y
    y_lo, core = mp // 2, mp % 2
    rows, features = width_operator.shape
    block = query_weight.shape[1]
    tokens = inputs.shape[0]

    def with_partner(value):
        other = shift(value, dy=1)
        return jnp.where(y == 0, jnp.concatenate([value, other], 0), jnp.concatenate([other, value], 0))

    operator = direct_gather(with_partner(width_operator), "dx", X, x, 0)
    weights = with_partner(jnp.concatenate([query_weight, output_weight], 1))
    weights = ring_gather(weights, "dz", Z, z, 0)
    operator, weights = lax.optimization_barrier((operator, weights))
    operator = ring_gather(operator, "dz", Z, z, 1)
    up, down = shift(weights, dx=1), shift(weights, dx=-1)
    half = Z // 2
    across = jnp.concatenate([shift(up[:half], dx=1), shift(down[half:], dx=-1)], 0)
    operator, up, down, across = lax.optimization_barrier((operator, up, down, across))
    operator = operator.reshape(-1, features)
    slabs = jnp.zeros((X,) + weights.shape, BF)
    for block_at, d in ((weights, 0), (up, -1), (down, 1), (across, 2)):
        slabs = put(slabs, block_at, 0, (x + d) % X)
    weights = slabs.reshape(-1, 2 * block)
    query_slab, output_slab = weights[:, :block], weights[:, block:]

    def contract(values):
        return mp_reduce(dot(values, operator, ((1,), (1,))).astype(BF), y_lo, core)

    def expand(values):
        return dot(values, operator, ((1,), (0,))).astype(BF)

    def project(low, slab, back, back_slab):
        whole = mp_gather(low, y_lo, core)
        back = mp_reduce(dot(back, back_slab, ((1,), (1,))).astype(BF), y_lo, core)
        low = dot(whole, slab, ((1,), (0,))).astype(BF)
        return low, back

    both = jnp.concatenate([inputs, upstream], 0)
    low = contract(both)
    low, back = project(low[:tokens], query_slab, low[tokens:], output_slab)
    query_and_back = mp_gather(jnp.concatenate([low, back], 0), y_lo, core)
    grown_both = expand(query_and_back)
    early = jnp.concatenate([query_and_back[tokens:].T, query_and_back[:tokens].T], 1)
    low = contract(grown_both)
    low, early = lax.optimization_barrier((low, early))
    low, back = project(low[:tokens], output_slab, low[tokens:], query_slab)
    late = lax.optimization_barrier(jnp.concatenate([back, low], 0).T)

    scale = 1.0 / math.sqrt(tokens * X * Z * Y)
    first_width = features * 3 // 8
    last_width = features - first_width
    part = Z * Y * rows
    ordered, *first = call_product(
        functools.partial(first_kernel, scale, first_width),
        jnp.stack([x, mp]),
        (*mp_blocks(late), early.reshape(X, part, -1), both, grown_both),
        [(X, part, 2 * tokens)] + [(part, first_width)] * X,
        3e-6,
    )
    ordered, first[1] = lax.optimization_barrier((ordered, first[1]))
    second = call_product(
        functools.partial(second_kernel, scale, last_width),
        z.reshape(1),
        (ordered.reshape(X, Z, Y * rows, -1), early.reshape(X, Z, Y * rows, -1), both, grown_both),
        [(X, Y * rows, last_width)] * Z,
        40e-6,
    )
    grown = dot(ordered.reshape(X * part, -1)[:, tokens:], operator, ((0,), (0,))).astype(BF)
    return scatter_gradient(first, second, grown, x, z, y)


def solution(mesh):
    return jax.shard_map(
        on_device,
        mesh=mesh,
        in_specs=(P("dp", "mp"), P("dp", "mp"), P("dp", "mp"), P("dp", "mp"), P("dp", "mp")),
        out_specs=(P("dp", "mp"), P("dp", "mp")),
        check_vma=False,
    )
```

```python
import functools
import math

import jax
import jax.numpy as jnp
from jax import lax
from jax.experimental import pallas as pl
from jax.experimental.layout import Layout, with_layout_constraint
from jax.experimental.pallas import tpu as pltpu
from jax.sharding import PartitionSpec as P

X, Z, Y = 4, 8, 2
BF = jnp.bfloat16
F32 = jnp.float32


def shift(value, dx=0, dz=0, dy=0):
    pairs = []
    for x in range(X):
        for z in range(Z):
            for y in range(Y):
                target = (((x + dx) % X) * Z + (z + dz) % Z) * Y + (y + dy) % Y
                pairs.append(((x * Z + z) * Y + y, target))
    return lax.ppermute(value, "dp", pairs)


def swap(value, bit):
    return lax.ppermute(value, "mp", [(i, i ^ bit) for i in range(4)])


def pair_swap_z(value):
    return lax.ppermute(value, "dp", [(i, i ^ Y) for i in range(X * Z * Y)])


def put(buffer, block, axis, index):
    starts = [0] * buffer.ndim
    starts[axis] = index
    return lax.dynamic_update_slice(buffer, jnp.expand_dims(block, axis), starts)


def ring_steps(block, axis_name, size):
    up = down = block
    for _ in range(1, size // 2):
        up, down = shift(up, **{axis_name: 1}), shift(down, **{axis_name: -1})
        yield up, down
    half = block.shape[0] // 2
    yield shift(up[:half], **{axis_name: 1}), shift(down[half:], **{axis_name: -1})


def place_ring(block, steps, size, me, axis):
    shape = block.shape[:axis] + (size,) + block.shape[axis:]
    out = put(jnp.zeros(shape, block.dtype), block, axis, me)
    for step, (up, down) in enumerate(steps, 1):
        if step == size // 2:
            return put(out, jnp.concatenate([up, down], 0), axis, (me + step) % size)
        out = put(out, up, axis, (me - step) % size)
        out = put(out, down, axis, (me + step) % size)


def direct_gather(block, axis_name, size, me, axis):
    shape = block.shape[:axis] + (size,) + block.shape[axis:]
    order = sorted(range(1, size), key=lambda d: -min(d, size - d))
    got = {d: shift(block, **{axis_name: d}) for d in order}
    out = put(jnp.zeros(shape, block.dtype), block, axis, me)
    for d in order:
        out = put(out, got[d], axis, (me - d) % size)
    return out


def dot(a, b, dims):
    return lax.dot_general(a, b, (dims, ((), ())), preferred_element_type=F32)


def columns(value, index, width):
    return lax.dynamic_slice_in_dim(value, index * width, width, 1)


def mp_reduce(partial, y_lo, core):
    rows, width = partial.shape[0], partial.shape[1] // 4
    order = (y_lo * 2, 2 - y_lo * 2)
    send = jnp.concatenate([columns(partial, o + 1 - core, width) for o in order], 0)
    keep = jnp.concatenate([columns(partial, o + core, width) for o in order], 0)
    total = keep.astype(F32) + swap(send, 1).astype(F32)
    other = swap(total[rows:].astype(BF), 2)
    return (total[:rows] + other.astype(F32)).astype(BF)


def mp_blocks(block):
    far = swap(block, 2)
    return [block, swap(block, 1), far, swap(far, 1)]


def mp_gather(block, y_lo, core):
    own, beside, far, diagonal = mp_blocks(block)
    first, low = core == 0, y_lo == 0
    near = jnp.where(first, own, beside), jnp.where(first, beside, own)
    away = jnp.where(first, far, diagonal), jnp.where(first, diagonal, far)
    return jnp.concatenate([jnp.where(low, n, a) for n, a in zip(near, away)] + [jnp.where(low, a, n) for n, a in zip(near, away)], 1)


def add(*values):
    total = values[0].astype(F32)
    for v in values[1:]:
        total = total + v.astype(F32)
    return total


def first_kernel(scale, width, position, own, beside, far, diagonal, early, both, grown, ordered, *blocks):
    for flipped, rows in enumerate((own, beside, far, diagonal)):
        ordered[position[1] ^ flipped] = rows[...]
    right = jnp.concatenate([both[:, :width], grown[:, :width]], 0)
    for d, block in enumerate(blocks):
        owner = lax.rem(position[0] + d, len(blocks))
        left = jnp.concatenate([ordered[owner], early[owner]], 1)
        total = lax.dot_general(left, right, (((1,), (0,)), ((), ())), preferred_element_type=F32)
        block[...] = (total * scale).astype(BF)


def second_kernel(scale, width, position, late, early, both, grown, *blocks):
    right = jnp.concatenate([both[:, -width:], grown[:, -width:]], 0)
    outer, _, rows, tokens = late.shape
    for d, block in enumerate(blocks):
        owner = lax.rem(position[0] + d, len(blocks))
        left = [side[:, owner].reshape(outer * rows, tokens) for side in (late, early)]
        total = lax.dot_general(
            jnp.concatenate(left, 1), right, (((1,), (0,)), ((), ())), preferred_element_type=F32
        )
        block[...] = (total * scale).astype(BF).reshape(block.shape)


def call_product(kernel, position, operands, shapes, seconds):
    vmem = pl.BlockSpec(memory_space=pltpu.VMEM)
    return pl.pallas_call(
        kernel,
        out_shape=[jax.ShapeDtypeStruct(shape, BF) for shape in shapes],
        in_specs=[pl.BlockSpec(memory_space=pltpu.SMEM)] + [pl.BlockSpec(v.shape) for v in operands],
        out_specs=[vmem] * len(shapes),
        compiler_params=pltpu.CompilerParams(vmem_limit_bytes=40 << 20),
        cost_estimate=pl.CostEstimate(
            flops=int(seconds * 1e15), bytes_accessed=int(seconds * 3e12), transcendentals=0
        ),
    )(position, *operands)


def direct_scatter(blocks, axis_name, stride=1):
    size = len(blocks)
    order = sorted(range(1, size), key=lambda d: -min(d, size - d))
    got = [shift(blocks[d], **{axis_name: d * stride}) for d in order]
    return add(blocks[0], *got)


def ring_scatter(blocks, axis_name, beside):
    size = len(blocks)
    far = size // 2
    half = blocks[0].shape[0] // 2
    up = shift(blocks[far][:half], **{axis_name: 1})
    down = shift(blocks[far][half:], **{axis_name: -1})
    for d in range(far - 1, 0, -1):
        a, b = blocks[d], blocks[-d]
        if d == far - 1:
            a = jnp.concatenate([add(a[:half], up).astype(BF), a[half:]], 0)
            b = jnp.concatenate([b[:half], add(b[half:], down).astype(BF)], 0)
        else:
            a, b = add(a, up).astype(BF), add(b, down).astype(BF)
        if d == 1:
            a, b, beside = lax.optimization_barrier((a, b, beside))
        up, down = shift(a, **{axis_name: 1}), shift(b, **{axis_name: -1})
    return add(blocks[0], up, down), beside


def by_owner(value, size, me):
    return [lax.dynamic_index_in_dim(value, (me + d) % size, 0, keepdims=False) for d in range(size)]


def scatter_gradient(first, second, grown, x, z, y):
    a = direct_scatter(first, "dx").astype(BF)
    b, (a, grown) = ring_scatter(second, "dz", (a, grown))
    b = direct_scatter(by_owner(b.astype(BF), X, x), "dx")
    a = a.reshape(Z // 2, 2, -1, a.shape[-1])
    odd = z % 2
    keep, send = (lax.dynamic_index_in_dim(a, i, 1, keepdims=False) for i in (odd, 1 - odd))
    a = add(keep, pair_swap_z(send)).astype(BF)
    a = direct_scatter(by_owner(a, Z // 2, z // 2), "dz", 2)
    both = jnp.concatenate([a, b], 1)
    both = both.reshape(Y, -1, both.shape[-1])
    send = lax.dynamic_index_in_dim(both, 1 - y, 0, keepdims=False).astype(BF)
    keep = lax.dynamic_index_in_dim(both, y, 0, keepdims=False)
    return grown, keep + shift(send, dy=1).astype(F32)


def on_device(inputs, upstream, width_operator, query_weight, output_weight):
    dp, mp = lax.axis_index("dp"), lax.axis_index("mp")
    x, z, y = dp // (Z * Y), dp // Y % Z, dp % Y
    y_lo, core = mp // 2, mp % 2
    rows, features = width_operator.shape
    block = query_weight.shape[1]
    tokens = inputs.shape[0]

    def with_partner(value):
        other = shift(value, dy=1)
        return jnp.where(y == 0, jnp.concatenate([value, other], 0), jnp.concatenate([other, value], 0))

    pair = with_partner(width_operator)
    steps = ring_steps(pair, "dz", Z)
    arrived = [next(steps) for _ in range(Z // 2 - 1)]
    weights = direct_gather(with_partner(jnp.concatenate([query_weight, output_weight], 1)), "dx", X, x, 0)
    arrived[-1], weights = lax.optimization_barrier((arrived[-1], weights))
    operator = place_ring(pair, arrived + list(steps), Z, z, 0)
    operator = place_ring(operator, ring_steps(operator, "dx", X), X, x, 0).reshape(-1, features)
    weights = place_ring(weights, ring_steps(weights, "dz", Z), Z, z, 1).reshape(-1, 2 * block)
    query_slab, output_slab = weights[:, :block], weights[:, block:]

    def contract(values):
        return mp_reduce(dot(values, operator, ((1,), (1,))).astype(BF), y_lo, core)

    def expand(values):
        return dot(values, operator, ((1,), (0,))).astype(BF)

    def project(low, slab, back, back_slab):
        whole = mp_gather(low, y_lo, core)
        back = mp_reduce(dot(back, back_slab, ((1,), (1,))).astype(BF), y_lo, core)
        low = dot(whole, slab, ((1,), (0,))).astype(BF)
        return low, back

    both = jnp.concatenate([inputs, upstream], 0)
    low = contract(both)
    low, back = project(low[:tokens], query_slab, low[tokens:], output_slab)
    query_and_back = mp_gather(jnp.concatenate([low, back], 0), y_lo, core)
    grown_both = expand(query_and_back)
    early = jnp.concatenate([query_and_back[tokens:].T, query_and_back[:tokens].T], 1)
    early = with_layout_constraint(early, Layout((0, 1)))
    low = contract(grown_both)
    low, early = lax.optimization_barrier((low, early))
    low, back = project(low[:tokens], output_slab, low[tokens:], query_slab)
    late = lax.optimization_barrier(jnp.concatenate([back, low], 0).T)

    scale = 1.0 / math.sqrt(tokens * X * Z * Y)
    first_width = features * 3 // 8
    last_width = features - first_width
    part = Z * Y * rows
    ordered, *first = call_product(
        functools.partial(first_kernel, scale, first_width),
        jnp.stack([x, mp]),
        (*mp_blocks(late), early.reshape(X, part, -1), both, grown_both),
        [(X, part, 2 * tokens)] + [(part, first_width)] * X,
        3e-6,
    )
    ordered, first[1] = lax.optimization_barrier((ordered, first[1]))
    second = call_product(
        functools.partial(second_kernel, scale, last_width),
        z.reshape(1),
        (ordered.reshape(X, Z, Y * rows, -1), early.reshape(X, Z, Y * rows, -1), both, grown_both),
        [(X, Y * rows, last_width)] * Z,
        40e-6,
    )
    grown = dot(ordered.reshape(X * part, -1)[:, tokens:], operator, ((0,), (0,))).astype(BF)
    return scatter_gradient(first, second, grown, x, z, y)


def solution(mesh):
    return jax.shard_map(
        on_device,
        mesh=mesh,
        in_specs=(P("dp", "mp"), P("dp", "mp"), P("dp", "mp"), P("dp", "mp"), P("dp", "mp")),
        out_specs=(P("dp", "mp"), P("dp", "mp")),
        check_vma=False,
    )
```

```python
import functools
import math

import jax
import jax.numpy as jnp
from jax import lax
from jax.experimental import pallas as pl
from jax.experimental.layout import Layout, with_layout_constraint
from jax.experimental.pallas import tpu as pltpu
from jax.sharding import PartitionSpec as P

X, Z, Y = 4, 8, 2
BF = jnp.bfloat16
F32 = jnp.float32


def shift(value, dx=0, dz=0, dy=0):
    pairs = []
    for x in range(X):
        for z in range(Z):
            for y in range(Y):
                target = (((x + dx) % X) * Z + (z + dz) % Z) * Y + (y + dy) % Y
                pairs.append(((x * Z + z) * Y + y, target))
    return lax.ppermute(value, "dp", pairs)


def swap(value, bit):
    return lax.ppermute(value, "mp", [(i, i ^ bit) for i in range(4)])


def pair_swap_z(value):
    return lax.ppermute(value, "dp", [(i, i ^ Y) for i in range(X * Z * Y)])


def put(buffer, block, axis, index):
    starts = [0] * buffer.ndim
    starts[axis] = index
    return lax.dynamic_update_slice(buffer, jnp.expand_dims(block, axis), starts)


def ring_steps(block, axis_name, size):
    up = down = block
    for _ in range(1, size // 2):
        up, down = shift(up, **{axis_name: 1}), shift(down, **{axis_name: -1})
        yield up, down
    half = block.shape[0] // 2
    yield shift(up[:half], **{axis_name: 1}), shift(down[half:], **{axis_name: -1})


def place_ring(block, steps, size, me, axis):
    shape = block.shape[:axis] + (size,) + block.shape[axis:]
    out = put(jnp.zeros(shape, block.dtype), block, axis, me)
    for step, (up, down) in enumerate(steps, 1):
        if step == size // 2:
            return put(out, jnp.concatenate([up, down], 0), axis, (me + step) % size)
        out = put(out, up, axis, (me - step) % size)
        out = put(out, down, axis, (me + step) % size)


def direct_gather(block, axis_name, size, me, axis):
    shape = block.shape[:axis] + (size,) + block.shape[axis:]
    order = sorted(range(1, size), key=lambda d: -min(d, size - d))
    got = {d: shift(block, **{axis_name: d}) for d in order}
    out = put(jnp.zeros(shape, block.dtype), block, axis, me)
    for d in order:
        out = put(out, got[d], axis, (me - d) % size)
    return out


def dot(a, b, dims):
    return lax.dot_general(a, b, (dims, ((), ())), preferred_element_type=F32)


def columns(value, index, width):
    return lax.dynamic_slice_in_dim(value, index * width, width, 1)


def mp_reduce(partial, y_lo, core):
    rows, width = partial.shape[0], partial.shape[1] // 4
    order = (y_lo * 2, 2 - y_lo * 2)
    send = jnp.concatenate([columns(partial, o + 1 - core, width) for o in order], 0)
    keep = jnp.concatenate([columns(partial, o + core, width) for o in order], 0)
    total = keep.astype(F32) + swap(send, 1).astype(F32)
    other = swap(total[rows:].astype(BF), 2)
    return (total[:rows] + other.astype(F32)).astype(BF)


def mp_blocks(block):
    far = swap(block, 2)
    return [block, swap(block, 1), far, swap(far, 1)]


def mp_gather(block, y_lo, core):
    own, beside, far, diagonal = mp_blocks(block)
    first, low = core == 0, y_lo == 0
    near = jnp.where(first, own, beside), jnp.where(first, beside, own)
    away = jnp.where(first, far, diagonal), jnp.where(first, diagonal, far)
    return jnp.concatenate([jnp.where(low, n, a) for n, a in zip(near, away)] + [jnp.where(low, a, n) for n, a in zip(near, away)], 1)


def add(*values):
    total = values[0].astype(F32)
    for v in values[1:]:
        total = total + v.astype(F32)
    return total


def last_kernel(scale, width, position, own, beside, far, diagonal, early, both, grown, ordered, *blocks):
    outer, inner, rows, tokens = ordered.shape
    for flipped, part in enumerate((own, beside, far, diagonal)):
        ordered[position[1] ^ flipped] = part[...].reshape(inner, rows, tokens)
    right = jnp.concatenate([both[:, -width:], grown[:, -width:]], 0)
    for d, block in enumerate(blocks):
        owner = lax.rem(position[0] + d, len(blocks))
        left = [side[:, owner].reshape(outer * rows, tokens) for side in (ordered, early)]
        total = lax.dot_general(
            jnp.concatenate(left, 1), right, (((1,), (0,)), ((), ())), preferred_element_type=F32
        )
        block[...] = (total * scale).astype(BF).reshape(block.shape)


def first_kernel(scale, width, position, late, early, both, grown, *blocks):
    right = jnp.concatenate([both[:, :width], grown[:, :width]], 0)
    for d, block in enumerate(blocks):
        owner = lax.rem(position[0] + d, len(blocks))
        left = jnp.concatenate([late[owner], early[owner]], 1)
        total = lax.dot_general(left, right, (((1,), (0,)), ((), ())), preferred_element_type=F32)
        block[...] = (total * scale).astype(BF)


def call_product(kernel, position, operands, shapes, seconds):
    vmem = pl.BlockSpec(memory_space=pltpu.VMEM)
    return pl.pallas_call(
        kernel,
        out_shape=[jax.ShapeDtypeStruct(shape, BF) for shape in shapes],
        in_specs=[pl.BlockSpec(memory_space=pltpu.SMEM)] + [pl.BlockSpec(v.shape) for v in operands],
        out_specs=[vmem] * len(shapes),
        compiler_params=pltpu.CompilerParams(vmem_limit_bytes=20 << 20),
        cost_estimate=pl.CostEstimate(
            flops=int(seconds * 1e15), bytes_accessed=int(seconds * 3e12), transcendentals=0
        ),
    )(position, *operands)


def direct_scatter(blocks, axis_name, stride=1):
    size = len(blocks)
    order = sorted(range(1, size), key=lambda d: -min(d, size - d))
    got = [shift(blocks[d], **{axis_name: d * stride}) for d in order]
    return add(blocks[0], *got)


def ring_scatter(blocks, axis_name, beside):
    size = len(blocks)
    far = size // 2
    half = blocks[0].shape[0] // 2
    up = shift(blocks[far][:half], **{axis_name: 1})
    down = shift(blocks[far][half:], **{axis_name: -1})
    for d in range(far - 1, 0, -1):
        a, b = blocks[d], blocks[-d]
        if d == far - 1:
            a = jnp.concatenate([add(a[:half], up).astype(BF), a[half:]], 0)
            b = jnp.concatenate([b[:half], add(b[half:], down).astype(BF)], 0)
        else:
            a, b = add(a, up).astype(BF), add(b, down).astype(BF)
        if d == 1:
            a, b, beside = lax.optimization_barrier((a, b, beside))
        up, down = shift(a, **{axis_name: 1}), shift(b, **{axis_name: -1})
    return add(blocks[0], up, down), beside


def by_owner(value, size, me):
    return [lax.dynamic_index_in_dim(value, (me + d) % size, 0, keepdims=False) for d in range(size)]


def scatter_gradient(first, second, grown, x, z, y):
    a = direct_scatter(first, "dx").astype(BF)
    b, (a, grown) = ring_scatter(second, "dz", (a, grown))
    b = direct_scatter(by_owner(b.astype(BF), X, x), "dx")
    a = a.reshape(Z // 2, 2, -1, a.shape[-1])
    odd = z % 2
    keep, send = (lax.dynamic_index_in_dim(a, i, 1, keepdims=False) for i in (odd, 1 - odd))
    a = add(keep, pair_swap_z(send)).astype(BF)
    a = direct_scatter(by_owner(a, Z // 2, z // 2), "dz", 2)
    both = jnp.concatenate([a, b], 1)
    both = both.reshape(Y, -1, both.shape[-1])
    send = lax.dynamic_index_in_dim(both, 1 - y, 0, keepdims=False).astype(BF)
    keep = lax.dynamic_index_in_dim(both, y, 0, keepdims=False)
    return grown, keep + shift(send, dy=1).astype(F32)


def on_device(inputs, upstream, width_operator, query_weight, output_weight):
    dp, mp = lax.axis_index("dp"), lax.axis_index("mp")
    x, z, y = dp // (Z * Y), dp // Y % Z, dp % Y
    y_lo, core = mp // 2, mp % 2
    rows, features = width_operator.shape
    block = query_weight.shape[1]
    tokens = inputs.shape[0]

    def with_partner(value):
        other = shift(value, dy=1)
        return jnp.where(y == 0, jnp.concatenate([value, other], 0), jnp.concatenate([other, value], 0))

    pair = with_partner(width_operator)
    opposite = shift(pair, dz=Z // 2)
    steps = ring_steps(pair, "dz", Z)
    arrived = [next(steps) for _ in range(Z // 2 - 1)]
    weights = direct_gather(with_partner(jnp.concatenate([query_weight, output_weight], 1)), "dx", X, x, 0)
    arrived[-1], weights = lax.optimization_barrier((arrived[-1], weights))
    middle = pair.shape[0] // 2
    operator = place_ring(pair, arrived + [(opposite[:middle], opposite[middle:])], Z, z, 0)
    operator = place_ring(operator, ring_steps(operator, "dx", X), X, x, 0).reshape(-1, features)
    weights = place_ring(weights, ring_steps(weights, "dz", Z), Z, z, 1).reshape(-1, 2 * block)
    query_slab, output_slab = weights[:, :block], weights[:, block:]

    def contract(values):
        return mp_reduce(dot(values, operator, ((1,), (1,))).astype(BF), y_lo, core)

    def expand(values):
        return dot(values, operator, ((1,), (0,))).astype(BF)

    def project(low, slab, back, back_slab):
        whole = mp_gather(low, y_lo, core)
        back = mp_reduce(dot(back, back_slab, ((1,), (1,))).astype(BF), y_lo, core)
        low = dot(whole, slab, ((1,), (0,))).astype(BF)
        return low, back

    both = jnp.concatenate([inputs, upstream], 0)
    low = contract(both)
    low, back = project(low[:tokens], query_slab, low[tokens:], output_slab)
    query_and_back = mp_gather(jnp.concatenate([low, back], 0), y_lo, core)
    grown_both = expand(query_and_back)
    early = jnp.concatenate([query_and_back[tokens:].T, query_and_back[:tokens].T], 1)
    early = with_layout_constraint(early, Layout((0, 1)))
    low = contract(grown_both)
    low, early = lax.optimization_barrier((low, early))
    low, back = project(low[:tokens], output_slab, low[tokens:], query_slab)
    late = lax.optimization_barrier(jnp.concatenate([back, low], 0).T)

    scale = 1.0 / math.sqrt(tokens * X * Z * Y)
    first_width = features * 3 // 8
    last_width = features - first_width
    part = Z * Y * rows
    ordered, *second = call_product(
        functools.partial(last_kernel, scale, last_width),
        jnp.stack([z, mp]),
        (*mp_blocks(late), early.reshape(X, Z, Y * rows, -1), both, grown_both),
        [(X, Z, Y * rows, 2 * tokens)] + [(X, Y * rows, last_width)] * Z,
        3e-6,
    )
    first = call_product(
        functools.partial(first_kernel, scale, first_width),
        x.reshape(1),
        (ordered.reshape(X, part, -1), early.reshape(X, part, -1), both, grown_both),
        [(part, first_width)] * X,
        3e-6,
    )
    grown = dot(ordered.reshape(X * part, -1)[:, tokens:], operator, ((0,), (0,))).astype(BF)
    return scatter_gradient(first, second, grown, x, z, y)


def solution(mesh):
    return jax.shard_map(
        on_device,
        mesh=mesh,
        in_specs=(P("dp", "mp"), P("dp", "mp"), P("dp", "mp"), P("dp", "mp"), P("dp", "mp")),
        out_specs=(P("dp", "mp"), P("dp", "mp")),
        check_vma=False,
    )
```

```python
import functools
import math

import jax
import jax.numpy as jnp
from jax import lax
from jax.experimental import pallas as pl
from jax.experimental.layout import Layout, with_layout_constraint
from jax.experimental.pallas import tpu as pltpu
from jax.sharding import PartitionSpec as P

X, Z, Y = 4, 8, 2
BF = jnp.bfloat16
F32 = jnp.float32


def shift(value, dx=0, dz=0, dy=0):
    pairs = []
    for x in range(X):
        for z in range(Z):
            for y in range(Y):
                target = (((x + dx) % X) * Z + (z + dz) % Z) * Y + (y + dy) % Y
                pairs.append(((x * Z + z) * Y + y, target))
    return lax.ppermute(value, "dp", pairs)


def swap(value, bit):
    return lax.ppermute(value, "mp", [(i, i ^ bit) for i in range(4)])


def pair_swap_z(value):
    return lax.ppermute(value, "dp", [(i, i ^ Y) for i in range(X * Z * Y)])


def put(buffer, block, axis, index):
    starts = [0] * buffer.ndim
    starts[axis] = index
    return lax.dynamic_update_slice(buffer, jnp.expand_dims(block, axis), starts)


def ring_steps(block, axis_name, size):
    up = down = block
    for _ in range(1, size // 2):
        up, down = shift(up, **{axis_name: 1}), shift(down, **{axis_name: -1})
        yield up, down
    half = block.shape[0] // 2
    yield shift(up[:half], **{axis_name: 1}), shift(down[half:], **{axis_name: -1})


def place_ring(block, steps, size, me, axis):
    shape = block.shape[:axis] + (size,) + block.shape[axis:]
    out = put(jnp.zeros(shape, block.dtype), block, axis, me)
    for step, (up, down) in enumerate(steps, 1):
        if step == size // 2:
            return put(out, jnp.concatenate([up, down], 0), axis, (me + step) % size)
        out = put(out, up, axis, (me - step) % size)
        out = put(out, down, axis, (me + step) % size)


def direct_gather(block, axis_name, size, me, axis):
    shape = block.shape[:axis] + (size,) + block.shape[axis:]
    order = sorted(range(1, size), key=lambda d: -min(d, size - d))
    got = {d: shift(block, **{axis_name: d}) for d in order}
    out = put(jnp.zeros(shape, block.dtype), block, axis, me)
    for d in order:
        out = put(out, got[d], axis, (me - d) % size)
    return out


def dot(a, b, dims):
    return lax.dot_general(a, b, (dims, ((), ())), preferred_element_type=F32)


def columns(value, index, width):
    return lax.dynamic_slice_in_dim(value, index * width, width, 1)


def core_sum(partial, y_lo, core, passenger=None):
    width = partial.shape[1] // 4
    order = (2 - y_lo * 2, y_lo * 2)
    send = [columns(partial, o + 1 - core, width) for o in order]
    keep = jnp.concatenate([columns(partial, o + core, width) for o in order], 0)
    rows = keep.shape[0]
    got = swap(jnp.concatenate(send if passenger is None else send + [passenger], 0), 1)
    return keep.astype(F32) + got[:rows].astype(F32), got[rows:]


def mp_order(own, beside, far, diagonal, y_lo, core):
    first, low = core == 0, y_lo == 0
    near = jnp.where(first, own, beside), jnp.where(first, beside, own)
    away = jnp.where(first, far, diagonal), jnp.where(first, diagonal, far)
    return jnp.concatenate([jnp.where(low, n, a) for n, a in zip(near, away)] + [jnp.where(low, a, n) for n, a in zip(near, away)], 1)


def add(*values):
    total = values[0].astype(F32)
    for v in values[1:]:
        total = total + v.astype(F32)
    return total


def last_kernel(scale, width, position, ours, theirs, early, both, grown, ordered, *blocks):
    outer, inner, rows, tokens = ordered.shape
    part = inner * rows
    for flipped, (side, at) in enumerate(((ours, 0), (theirs, 0), (ours, part), (theirs, part))):
        ordered[position[1] ^ flipped] = side[at : at + part].reshape(inner, rows, tokens)
    right = jnp.concatenate([both[:, -width:], grown[:, -width:]], 0)
    for d, block in enumerate(blocks):
        owner = lax.rem(position[0] + d, len(blocks))
        left = [side[:, owner].reshape(outer * rows, tokens) for side in (ordered, early)]
        total = lax.dot_general(
            jnp.concatenate(left, 1), right, (((1,), (0,)), ((), ())), preferred_element_type=F32
        )
        block[...] = (total * scale).astype(BF).reshape(block.shape)


def first_kernel(scale, width, position, late, early, both, grown, *blocks):
    right = jnp.concatenate([both[:, :width], grown[:, :width]], 0)
    for d, block in enumerate(blocks):
        owner = lax.rem(position[0] + d, len(blocks))
        left = jnp.concatenate([late[owner], early[owner]], 1)
        total = lax.dot_general(left, right, (((1,), (0,)), ((), ())), preferred_element_type=F32)
        block[...] = (total * scale).astype(BF)


def call_product(kernel, position, operands, shapes, seconds):
    vmem = pl.BlockSpec(memory_space=pltpu.VMEM)
    return pl.pallas_call(
        kernel,
        out_shape=[jax.ShapeDtypeStruct(shape, BF) for shape in shapes],
        in_specs=[pl.BlockSpec(memory_space=pltpu.SMEM)] + [pl.BlockSpec(v.shape) for v in operands],
        out_specs=[vmem] * len(shapes),
        compiler_params=pltpu.CompilerParams(vmem_limit_bytes=12 << 20),
        cost_estimate=pl.CostEstimate(
            flops=int(seconds * 1e15), bytes_accessed=int(seconds * 3e12), transcendentals=0
        ),
    )(position, *operands)


def direct_scatter(blocks, axis_name, stride=1):
    size = len(blocks)
    order = sorted(range(1, size), key=lambda d: -min(d, size - d))
    got = [shift(blocks[d], **{axis_name: d * stride}) for d in order]
    return add(blocks[0], *got)


def ring_scatter(blocks, axis_name, beside):
    size = len(blocks)
    far = size // 2
    half = blocks[0].shape[0] // 2
    up = shift(blocks[far][:half], **{axis_name: 1})
    down = shift(blocks[far][half:], **{axis_name: -1})
    for d in range(far - 1, 0, -1):
        a, b = blocks[d], blocks[-d]
        if d == far - 1:
            a = jnp.concatenate([add(a[:half], up).astype(BF), a[half:]], 0)
            b = jnp.concatenate([b[:half], add(b[half:], down).astype(BF)], 0)
        else:
            a, b = add(a, up).astype(BF), add(b, down).astype(BF)
        if d == 1:
            a, b, beside = lax.optimization_barrier((a, b, beside))
        up, down = shift(a, **{axis_name: 1}), shift(b, **{axis_name: -1})
    return add(blocks[0], up, down), beside


def by_owner(value, size, me):
    return [lax.dynamic_index_in_dim(value, (me + d) % size, 0, keepdims=False) for d in range(size)]


def scatter_gradient(first, second, grown, x, z, y):
    rows = first[0].shape[0] // (Z * Y)
    a = direct_scatter(first, "dx").astype(BF)
    b, (a, grown) = ring_scatter(second, "dz", (a, grown))
    a = a.reshape(Z, Y, rows, -1)
    keep, send = (lax.dynamic_index_in_dim(a, i, 1, keepdims=False) for i in (y, 1 - y))
    a = add(keep, shift(send, dy=1)).astype(BF).reshape(Z // 2, 2, rows, -1)
    odd = z % 2
    keep, send = (lax.dynamic_index_in_dim(a, i, 1, keepdims=False) for i in (odd, 1 - odd))
    a = add(keep, pair_swap_z(send)).astype(BF)
    b = direct_scatter(by_owner(b.astype(BF), X, x), "dx").reshape(Y, rows, -1)
    a = direct_scatter(by_owner(a, Z // 2, z // 2), "dz", 2)
    keep, send = (lax.dynamic_index_in_dim(b, i, 0, keepdims=False) for i in (y, 1 - y))
    b = add(keep, shift(send.astype(BF), dy=1))
    return grown, jnp.concatenate([a, b], 1)


def on_device(inputs, upstream, width_operator, query_weight, output_weight):
    dp, mp = lax.axis_index("dp"), lax.axis_index("mp")
    x, z, y = dp // (Z * Y), dp // Y % Z, dp % Y
    y_lo, core = mp // 2, mp % 2
    rows, features = width_operator.shape
    block = query_weight.shape[1]
    tokens = inputs.shape[0]

    def with_partner(value):
        other = shift(value, dy=1)
        return jnp.where(y == 0, jnp.concatenate([value, other], 0), jnp.concatenate([other, value], 0))

    pair = with_partner(width_operator)
    opposite = shift(pair, dz=Z // 2)
    steps = ring_steps(pair, "dz", Z)
    arrived = [next(steps) for _ in range(Z // 2 - 1)]
    weights = direct_gather(with_partner(jnp.concatenate([query_weight, output_weight], 1)), "dx", X, x, 0)
    arrived[-1], weights = lax.optimization_barrier((arrived[-1], weights))
    middle = pair.shape[0] // 2
    operator = place_ring(pair, arrived + [(opposite[:middle], opposite[middle:])], Z, z, 0)
    operator = place_ring(operator, ring_steps(operator, "dx", X), X, x, 0).reshape(-1, features)
    weights = place_ring(weights, ring_steps(weights, "dz", Z), Z, z, 1).reshape(-1, 2 * block)
    query_slab, output_slab = weights[:, :block], weights[:, block:]

    def contract(values):
        total, _ = core_sum(dot(values, operator, ((1,), (1,))).astype(BF), y_lo, core)
        got = swap(total[: 3 * tokens].astype(BF), 2)
        near = add(total[2 * tokens :], got[: 2 * tokens]).astype(BF)
        far = add(total[:tokens], got[2 * tokens :]).astype(BF)
        return near, far

    def expand(values):
        return dot(values, operator, ((1,), (0,))).astype(BF)

    def project(near, far, slab, back_slab, turn):
        pair = jnp.concatenate([near[:tokens], far], 0)
        back, beside = core_sum(dot(near[tokens:], back_slab, ((1,), (1,))).astype(BF), y_lo, core, pair)
        back = lax.optimization_barrier(back.astype(BF))
        got = swap(back, 2)
        near_back, far_back = add(back[tokens:], got[:tokens]).astype(BF), add(back[:tokens], got[tokens:]).astype(BF)
        whole = mp_order(near[:tokens], beside[:tokens], far, beside[tokens:], y_lo, core)
        low = dot(whole, slab, ((1,), (0,))).astype(BF)
        low_far = swap(low, 2)
        own, away = jnp.concatenate([near_back, low], 0), jnp.concatenate([far_back, low_far], 0)
        ours = jnp.concatenate([own.T, away.T] if turn else [own, away], 0)
        return ours, swap(ours, 1)

    both = jnp.concatenate([inputs, upstream], 0)
    near, far = contract(both)
    ours, theirs = project(near, far, query_slab, output_slab, False)
    count = 2 * tokens
    back_and_query = mp_order(ours[:count], theirs[:count], ours[count:], theirs[count:], y_lo, core)
    grown_both = expand(jnp.concatenate([back_and_query[tokens:], back_and_query[:tokens]], 0))
    early = back_and_query.T
    early = with_layout_constraint(early, Layout((0, 1)))
    near, far = contract(grown_both)
    near, early = lax.optimization_barrier((near, early))
    late = project(near, far, output_slab, query_slab, True)

    scale = 1.0 / math.sqrt(tokens * X * Z * Y)
    first_width = features * 3 // 8
    last_width = features - first_width
    part = Z * Y * rows
    ordered, *second = call_product(
        functools.partial(last_kernel, scale, last_width),
        jnp.stack([z, mp]),
        (*late, early.reshape(X, Z, Y * rows, -1), both, grown_both),
        [(X, Z, Y * rows, 2 * tokens)] + [(X, Y * rows, last_width)] * Z,
        3e-6,
    )
    first = call_product(
        functools.partial(first_kernel, scale, first_width),
        x.reshape(1),
        (ordered.reshape(X, part, -1), early.reshape(X, part, -1), both, grown_both),
        [(part, first_width)] * X,
        3e-6,
    )
    grown = dot(ordered.reshape(X * part, -1)[:, tokens:], operator, ((0,), (0,))).astype(BF)
    return scatter_gradient(first, second, grown, x, z, y)


def solution(mesh):
    return jax.shard_map(
        on_device,
        mesh=mesh,
        in_specs=(P("dp", "mp"), P("dp", "mp"), P("dp", "mp"), P("dp", "mp"), P("dp", "mp")),
        out_specs=(P("dp", "mp"), P("dp", "mp")),
        check_vma=False,
    )
```

```python
import functools
import math

import jax
import jax.numpy as jnp
from jax import lax
from jax.experimental import pallas as pl
from jax.experimental.layout import Layout, with_layout_constraint
from jax.experimental.pallas import tpu as pltpu
from jax.sharding import PartitionSpec as P

X, Z, Y = 4, 8, 2
BF = jnp.bfloat16
F32 = jnp.float32


def shift(value, dx=0, dz=0, dy=0):
    pairs = []
    for x in range(X):
        for z in range(Z):
            for y in range(Y):
                target = (((x + dx) % X) * Z + (z + dz) % Z) * Y + (y + dy) % Y
                pairs.append(((x * Z + z) * Y + y, target))
    return lax.ppermute(value, "dp", pairs)


def swap(value, bit):
    return lax.ppermute(value, "mp", [(i, i ^ bit) for i in range(4)])


def pair_swap_z(value):
    return lax.ppermute(value, "dp", [(i, i ^ Y) for i in range(X * Z * Y)])


def put(buffer, block, axis, index):
    starts = [0] * buffer.ndim
    starts[axis] = index
    return lax.dynamic_update_slice(buffer, jnp.expand_dims(block, axis), starts)


def ring_steps(block, axis_name, size):
    up = down = block
    for _ in range(1, size // 2):
        up, down = shift(up, **{axis_name: 1}), shift(down, **{axis_name: -1})
        yield up, down
    half = block.shape[0] // 2
    yield shift(up[:half], **{axis_name: 1}), shift(down[half:], **{axis_name: -1})


def place_ring(block, steps, size, me, axis):
    shape = block.shape[:axis] + (size,) + block.shape[axis:]
    out = put(jnp.zeros(shape, block.dtype), block, axis, me)
    for step, (up, down) in enumerate(steps, 1):
        if step == size // 2:
            return put(out, jnp.concatenate([up, down], 0), axis, (me + step) % size)
        out = put(out, up, axis, (me - step) % size)
        out = put(out, down, axis, (me + step) % size)


def direct_gather(block, axis_name, size, me, axis):
    shape = block.shape[:axis] + (size,) + block.shape[axis:]
    order = sorted(range(1, size), key=lambda d: -min(d, size - d))
    got = {d: shift(block, **{axis_name: d}) for d in order}
    out = put(jnp.zeros(shape, block.dtype), block, axis, me)
    for d in order:
        out = put(out, got[d], axis, (me - d) % size)
    return out


def dot(a, b, dims):
    return lax.dot_general(a, b, (dims, ((), ())), preferred_element_type=F32)


def columns(value, index, width):
    return lax.dynamic_slice_in_dim(value, index * width, width, 1)


def core_sum(partial, y_lo, core):
    width = partial.shape[1] // 4
    order = (2 - y_lo * 2, y_lo * 2)
    send = jnp.concatenate([columns(partial, o + 1 - core, width) for o in order], 0)
    keep = jnp.concatenate([columns(partial, o + core, width) for o in order], 0)
    return keep.astype(F32) + swap(send, 1).astype(F32)


def mp_order(own, beside, far, diagonal, y_lo, core):
    first, low = core == 0, y_lo == 0
    near = jnp.where(first, own, beside), jnp.where(first, beside, own)
    away = jnp.where(first, far, diagonal), jnp.where(first, diagonal, far)
    return jnp.concatenate([jnp.where(low, n, a) for n, a in zip(near, away)] + [jnp.where(low, a, n) for n, a in zip(near, away)], 1)


def add(*values):
    total = values[0].astype(F32)
    for v in values[1:]:
        total = total + v.astype(F32)
    return total


def last_kernel(scale, width, position, ours, theirs, early, both, grown, ordered, *blocks):
    outer, inner, rows, tokens = ordered.shape
    part = inner * rows
    for flipped, (side, at) in enumerate(((ours, 0), (theirs, 0), (ours, part), (theirs, part))):
        ordered[position[1] ^ flipped] = side[at : at + part].reshape(inner, rows, tokens)
    right = jnp.concatenate([both[:, -width:], grown[:, -width:]], 0)
    for d, block in enumerate(blocks):
        owner = lax.rem(position[0] + d, len(blocks))
        left = [side[:, owner].reshape(outer * rows, tokens) for side in (ordered, early)]
        total = lax.dot_general(
            jnp.concatenate(left, 1), right, (((1,), (0,)), ((), ())), preferred_element_type=F32
        )
        block[...] = (total * scale).astype(BF).reshape(block.shape)


def first_kernel(scale, width, position, late, early, both, grown, *blocks):
    right = jnp.concatenate([both[:, :width], grown[:, :width]], 0)
    for d, block in enumerate(blocks):
        owner = lax.rem(position[0] + d, len(blocks))
        left = jnp.concatenate([late[owner], early[owner]], 1)
        total = lax.dot_general(left, right, (((1,), (0,)), ((), ())), preferred_element_type=F32)
        block[...] = (total * scale).astype(BF)


def call_product(kernel, position, operands, shapes, seconds):
    vmem = pl.BlockSpec(memory_space=pltpu.VMEM)
    return pl.pallas_call(
        kernel,
        out_shape=[jax.ShapeDtypeStruct(shape, BF) for shape in shapes],
        in_specs=[pl.BlockSpec(memory_space=pltpu.SMEM)] + [pl.BlockSpec(v.shape) for v in operands],
        out_specs=[vmem] * len(shapes),
        compiler_params=pltpu.CompilerParams(vmem_limit_bytes=12 << 20),
        cost_estimate=pl.CostEstimate(
            flops=int(seconds * 1e15), bytes_accessed=int(seconds * 3e12), transcendentals=0
        ),
    )(position, *operands)


def direct_scatter(blocks, axis_name, stride=1):
    size = len(blocks)
    order = sorted(range(1, size), key=lambda d: -min(d, size - d))
    got = [shift(blocks[d], **{axis_name: d * stride}) for d in order]
    return add(blocks[0], *got)


def ring_scatter(blocks, axis_name, beside):
    size = len(blocks)
    far = size // 2
    half = blocks[0].shape[0] // 2
    up = shift(blocks[far][:half], **{axis_name: 1})
    down = shift(blocks[far][half:], **{axis_name: -1})
    for d in range(far - 1, 0, -1):
        a, b = blocks[d], blocks[-d]
        if d == far - 1:
            a = jnp.concatenate([add(a[:half], up).astype(BF), a[half:]], 0)
            b = jnp.concatenate([b[:half], add(b[half:], down).astype(BF)], 0)
        else:
            a, b = add(a, up).astype(BF), add(b, down).astype(BF)
        if d == 1:
            a, b, beside = lax.optimization_barrier((a, b, beside))
        up, down = shift(a, **{axis_name: 1}), shift(b, **{axis_name: -1})
    return add(blocks[0], up, down), beside


def by_owner(value, size, me):
    return [lax.dynamic_index_in_dim(value, (me + d) % size, 0, keepdims=False) for d in range(size)]


def scatter_gradient(first, second, grown, x, z, y):
    rows = first[0].shape[0] // (Z * Y)
    a = direct_scatter(first, "dx").astype(BF)
    b, (a, grown) = ring_scatter(second, "dz", (a, grown))
    a = a.reshape(Z, Y, rows, -1)
    keep, send = (lax.dynamic_index_in_dim(a, i, 1, keepdims=False) for i in (y, 1 - y))
    a = add(keep, shift(send, dy=1)).astype(BF).reshape(Z // 2, 2, rows, -1)
    odd = z % 2
    keep, send = (lax.dynamic_index_in_dim(a, i, 1, keepdims=False) for i in (odd, 1 - odd))
    a = add(keep, pair_swap_z(send)).astype(BF)
    b = direct_scatter(by_owner(b.astype(BF), X, x), "dx").reshape(Y, rows, -1)
    a = direct_scatter(by_owner(a, Z // 2, z // 2), "dz", 2)
    keep, send = (lax.dynamic_index_in_dim(b, i, 0, keepdims=False) for i in (y, 1 - y))
    b = add(keep, shift(send.astype(BF), dy=1))
    return grown, jnp.concatenate([a, b], 1)


def on_device(inputs, upstream, width_operator, query_weight, output_weight):
    dp, mp = lax.axis_index("dp"), lax.axis_index("mp")
    x, z, y = dp // (Z * Y), dp // Y % Z, dp % Y
    y_lo, core = mp // 2, mp % 2
    rows, features = width_operator.shape
    block = query_weight.shape[1]
    tokens = inputs.shape[0]

    def with_partner(value):
        other = shift(value, dy=1)
        return jnp.where(y == 0, jnp.concatenate([value, other], 0), jnp.concatenate([other, value], 0))

    pair = with_partner(width_operator)
    opposite = shift(pair, dz=Z // 2)
    steps = ring_steps(pair, "dz", Z)
    arrived = [next(steps) for _ in range(Z // 2 - 1)]
    weights = direct_gather(with_partner(jnp.concatenate([query_weight, output_weight], 1)), "dx", X, x, 0)
    arrived[-1], weights = lax.optimization_barrier((arrived[-1], weights))
    middle = pair.shape[0] // 2
    operator = place_ring(pair, arrived + [(opposite[:middle], opposite[middle:])], Z, z, 0)
    operator = place_ring(operator, ring_steps(operator, "dx", X), X, x, 0).reshape(-1, features)
    weights = place_ring(weights, ring_steps(weights, "dz", Z), Z, z, 1).reshape(-1, 2 * block)
    query_slab, output_slab = weights[:, :block], weights[:, block:]

    def contract(values):
        total = core_sum(dot(values, operator, ((1,), (1,))).astype(BF), y_lo, core)
        far_low, far_back, low, back = (total[i * tokens : (i + 1) * tokens] for i in range(4))
        back = add(back, swap(far_back.astype(BF), 2)).astype(BF)
        got = swap(jnp.concatenate([far_low, low], 0).astype(BF), 2)
        return add(low, got[:tokens]).astype(BF), add(far_low, got[tokens:]).astype(BF), back

    def expand(values):
        return dot(values, operator, ((1,), (0,))).astype(BF)

    def project(near, far, back, slab, back_slab, turn):
        back = core_sum(dot(back, back_slab, ((1,), (1,))).astype(BF), y_lo, core).astype(BF)
        got = swap(back, 2)
        back, near = lax.optimization_barrier((back, near))
        near_back, far_back = add(back[tokens:], got[:tokens]).astype(BF), add(back[:tokens], got[tokens:]).astype(BF)
        beside = swap(jnp.concatenate([near, far], 0), 1)
        whole = mp_order(near, beside[:tokens], far, beside[tokens:], y_lo, core)
        low = dot(whole, slab, ((1,), (0,))).astype(BF)
        low_far = swap(low, 2)
        own, away = jnp.concatenate([near_back, low], 0), jnp.concatenate([far_back, low_far], 0)
        ours = jnp.concatenate([own.T, away.T] if turn else [own, away], 0)
        return ours, swap(ours, 1)

    both = jnp.concatenate([inputs, upstream], 0)
    near, far, back = contract(both)
    ours, theirs = project(near, far, back, query_slab, output_slab, False)
    count = 2 * tokens
    back_and_query = mp_order(ours[:count], theirs[:count], ours[count:], theirs[count:], y_lo, core)
    grown_both = expand(jnp.concatenate([back_and_query[tokens:], back_and_query[:tokens]], 0))
    early = back_and_query.T
    early = with_layout_constraint(early, Layout((0, 1)))
    near, far, back = contract(grown_both)
    near, early = lax.optimization_barrier((near, early))
    late = project(near, far, back, output_slab, query_slab, True)

    scale = 1.0 / math.sqrt(tokens * X * Z * Y)
    first_width = features * 3 // 8
    last_width = features - first_width
    part = Z * Y * rows
    ordered, *second = call_product(
        functools.partial(last_kernel, scale, last_width),
        jnp.stack([z, mp]),
        (*late, early.reshape(X, Z, Y * rows, -1), both, grown_both),
        [(X, Z, Y * rows, 2 * tokens)] + [(X, Y * rows, last_width)] * Z,
        3e-6,
    )
    first = call_product(
        functools.partial(first_kernel, scale, first_width),
        x.reshape(1),
        (ordered.reshape(X, part, -1), early.reshape(X, part, -1), both, grown_both),
        [(part, first_width)] * X,
        3e-6,
    )
    grown = dot(ordered.reshape(X * part, -1)[:, tokens:], operator, ((0,), (0,))).astype(BF)
    return scatter_gradient(first, second, grown, x, z, y)


def solution(mesh):
    return jax.shard_map(
        on_device,
        mesh=mesh,
        in_specs=(P("dp", "mp"), P("dp", "mp"), P("dp", "mp"), P("dp", "mp"), P("dp", "mp")),
        out_specs=(P("dp", "mp"), P("dp", "mp")),
        check_vma=False,
    )
```

```python
import functools
import math

import jax
import jax.numpy as jnp
from jax import lax
from jax.experimental import pallas as pl
from jax.experimental.layout import Layout, with_layout_constraint
from jax.experimental.pallas import tpu as pltpu
from jax.sharding import PartitionSpec as P

X, Z, Y = 4, 8, 2
BF = jnp.bfloat16
F32 = jnp.float32


def shift(value, dx=0, dz=0, dy=0):
    pairs = []
    for x in range(X):
        for z in range(Z):
            for y in range(Y):
                target = (((x + dx) % X) * Z + (z + dz) % Z) * Y + (y + dy) % Y
                pairs.append(((x * Z + z) * Y + y, target))
    return lax.ppermute(value, "dp", pairs)


def swap(value, bit):
    return lax.ppermute(value, "mp", [(i, i ^ bit) for i in range(4)])


def pair_swap_z(value):
    return lax.ppermute(value, "dp", [(i, i ^ Y) for i in range(X * Z * Y)])


def put(buffer, block, axis, index):
    starts = [0] * buffer.ndim
    starts[axis] = index
    return lax.dynamic_update_slice(buffer, jnp.expand_dims(block, axis), starts)


def ring_steps(block, axis_name, size):
    up = down = block
    for _ in range(1, size // 2):
        up, down = shift(up, **{axis_name: 1}), shift(down, **{axis_name: -1})
        yield up, down
    half = block.shape[0] // 2
    yield shift(up[:half], **{axis_name: 1}), shift(down[half:], **{axis_name: -1})


def place_ring(block, steps, size, me, axis):
    shape = block.shape[:axis] + (size,) + block.shape[axis:]
    out = put(jnp.zeros(shape, block.dtype), block, axis, me)
    for step, (up, down) in enumerate(steps, 1):
        if step == size // 2:
            return put(out, jnp.concatenate([up, down], 0), axis, (me + step) % size)
        out = put(out, up, axis, (me - step) % size)
        out = put(out, down, axis, (me + step) % size)


def direct_gather(block, axis_name, size, me, axis):
    shape = block.shape[:axis] + (size,) + block.shape[axis:]
    order = sorted(range(1, size), key=lambda d: -min(d, size - d))
    got = {d: shift(block, **{axis_name: d}) for d in order}
    out = put(jnp.zeros(shape, block.dtype), block, axis, me)
    for d in order:
        out = put(out, got[d], axis, (me - d) % size)
    return out


def dot(a, b, dims):
    return lax.dot_general(a, b, (dims, ((), ())), preferred_element_type=F32)


def columns(value, index, width):
    return lax.dynamic_slice_in_dim(value, index * width, width, 1)


def core_sum(partial, y_lo, core):
    width = partial.shape[1] // 4
    order = (2 - y_lo * 2, y_lo * 2)
    send = jnp.concatenate([columns(partial, o + 1 - core, width) for o in order], 0)
    keep = jnp.concatenate([columns(partial, o + core, width) for o in order], 0)
    return keep.astype(F32) + swap(send, 1).astype(F32)


def mp_order(own, beside, far, diagonal, y_lo, core):
    first, low = core == 0, y_lo == 0
    near = jnp.where(first, own, beside), jnp.where(first, beside, own)
    away = jnp.where(first, far, diagonal), jnp.where(first, diagonal, far)
    return jnp.concatenate([jnp.where(low, n, a) for n, a in zip(near, away)] + [jnp.where(low, a, n) for n, a in zip(near, away)], 1)


def add(*values):
    total = values[0].astype(F32)
    for v in values[1:]:
        total = total + v.astype(F32)
    return total


def last_kernel(scale, width, position, own, beside, far, diagonal, early, both, grown, ordered, *blocks):
    outer, inner, rows, tokens = ordered.shape
    for flipped, part in enumerate((own, beside, far, diagonal)):
        ordered[position[1] ^ flipped] = part[...].reshape(inner, rows, tokens)
    right = jnp.concatenate([both[:, -width:], grown[:, -width:]], 0)
    for d, block in enumerate(blocks):
        owner = lax.rem(position[0] + d, len(blocks))
        left = [side[:, owner].reshape(outer * rows, tokens) for side in (ordered, early)]
        total = lax.dot_general(
            jnp.concatenate(left, 1), right, (((1,), (0,)), ((), ())), preferred_element_type=F32
        )
        block[...] = (total * scale).astype(BF).reshape(block.shape)


def first_kernel(scale, width, position, late, early, both, grown, *blocks):
    right = jnp.concatenate([both[:, :width], grown[:, :width]], 0)
    for d, block in enumerate(blocks):
        owner = lax.rem(position[0] + d, len(blocks))
        left = jnp.concatenate([late[owner], early[owner]], 1)
        total = lax.dot_general(left, right, (((1,), (0,)), ((), ())), preferred_element_type=F32)
        block[...] = (total * scale).astype(BF)


def call_product(kernel, position, operands, shapes, seconds):
    vmem = pl.BlockSpec(memory_space=pltpu.VMEM)
    return pl.pallas_call(
        kernel,
        out_shape=[jax.ShapeDtypeStruct(shape, BF) for shape in shapes],
        in_specs=[pl.BlockSpec(memory_space=pltpu.SMEM)] + [pl.BlockSpec(v.shape) for v in operands],
        out_specs=[vmem] * len(shapes),
        compiler_params=pltpu.CompilerParams(vmem_limit_bytes=12 << 20),
        cost_estimate=pl.CostEstimate(
            flops=int(seconds * 1e15), bytes_accessed=int(seconds * 3e12), transcendentals=0
        ),
    )(position, *operands)


def direct_scatter(blocks, axis_name, stride=1):
    size = len(blocks)
    order = sorted(range(1, size), key=lambda d: -min(d, size - d))
    got = [shift(blocks[d], **{axis_name: d * stride}) for d in order]
    return add(blocks[0], *got)


def ring_scatter(blocks, axis_name, beside):
    size = len(blocks)
    far = size // 2
    half = blocks[0].shape[0] // 2
    up = shift(blocks[far][:half], **{axis_name: 1})
    down = shift(blocks[far][half:], **{axis_name: -1})
    for d in range(far - 1, 0, -1):
        a, b = blocks[d], blocks[-d]
        if d == far - 1:
            a = jnp.concatenate([add(a[:half], up).astype(BF), a[half:]], 0)
            b = jnp.concatenate([b[:half], add(b[half:], down).astype(BF)], 0)
        else:
            a, b = add(a, up).astype(BF), add(b, down).astype(BF)
        if d == 1:
            a, b, beside = lax.optimization_barrier((a, b, beside))
        up, down = shift(a, **{axis_name: 1}), shift(b, **{axis_name: -1})
    return add(blocks[0], up, down), beside


def by_owner(value, size, me):
    return [lax.dynamic_index_in_dim(value, (me + d) % size, 0, keepdims=False) for d in range(size)]


def scatter_gradient(first, second, grown, x, z, y):
    rows = first[0].shape[0] // (Z * Y)
    a = direct_scatter(first, "dx").astype(BF)
    b, (a, grown) = ring_scatter(second, "dz", (a, grown))
    a = a.reshape(Z, Y, rows, -1)
    keep, send = (lax.dynamic_index_in_dim(a, i, 1, keepdims=False) for i in (y, 1 - y))
    a = add(keep, shift(send, dy=1)).astype(BF).reshape(Z // 2, 2, rows, -1)
    odd = z % 2
    keep, send = (lax.dynamic_index_in_dim(a, i, 1, keepdims=False) for i in (odd, 1 - odd))
    a = add(keep, pair_swap_z(send)).astype(BF)
    b = direct_scatter(by_owner(b.astype(BF), X, x), "dx").reshape(Y, rows, -1)
    a = direct_scatter(by_owner(a, Z // 2, z // 2), "dz", 2)
    keep, send = (lax.dynamic_index_in_dim(b, i, 0, keepdims=False) for i in (y, 1 - y))
    b = add(keep, shift(send.astype(BF), dy=1))
    return grown, jnp.concatenate([a, b], 1)


def on_device(inputs, upstream, width_operator, query_weight, output_weight):
    dp, mp = lax.axis_index("dp"), lax.axis_index("mp")
    x, z, y = dp // (Z * Y), dp // Y % Z, dp % Y
    y_lo, core = mp // 2, mp % 2
    rows, features = width_operator.shape
    block = query_weight.shape[1]
    tokens = inputs.shape[0]

    def with_partner(value):
        other = shift(value, dy=1)
        return jnp.where(y == 0, jnp.concatenate([value, other], 0), jnp.concatenate([other, value], 0))

    pair = with_partner(width_operator)
    opposite = shift(pair, dz=Z // 2)
    steps = ring_steps(pair, "dz", Z)
    arrived = [next(steps) for _ in range(Z // 2 - 1)]
    weights = direct_gather(with_partner(jnp.concatenate([query_weight, output_weight], 1)), "dx", X, x, 0)
    arrived[-1], weights = lax.optimization_barrier((arrived[-1], weights))
    middle = pair.shape[0] // 2
    operator = place_ring(pair, arrived + [(opposite[:middle], opposite[middle:])], Z, z, 0)
    operator = place_ring(operator, ring_steps(operator, "dx", X), X, x, 0).reshape(-1, features)
    weights = place_ring(weights, ring_steps(weights, "dz", Z), Z, z, 1).reshape(-1, 2 * block)
    query_slab, output_slab = weights[:, :block], weights[:, block:]

    def contract(values):
        total = core_sum(dot(values, operator, ((1,), (1,))).astype(BF), y_lo, core)
        far_low, far_back, low, back = (total[i * tokens : (i + 1) * tokens] for i in range(4))
        back = add(back, swap(far_back.astype(BF), 2)).astype(BF)
        got = swap(jnp.concatenate([far_low, low], 0).astype(BF), 2)
        return add(low, got[:tokens]).astype(BF), add(far_low, got[tokens:]).astype(BF), back

    def expand(values):
        return dot(values, operator, ((1,), (0,))).astype(BF)

    def project(near, far, back, slab, back_slab, turn):
        back = core_sum(dot(back, back_slab, ((1,), (1,))).astype(BF), y_lo, core).astype(BF)
        got = swap(back, 2)
        back, near = lax.optimization_barrier((back, near))
        near_back, far_back = add(back[tokens:], got[:tokens]).astype(BF), add(back[:tokens], got[tokens:]).astype(BF)
        beside = swap(jnp.concatenate([near, far], 0), 1)
        whole = mp_order(near, beside[:tokens], far, beside[tokens:], y_lo, core)
        low = dot(whole, slab, ((1,), (0,))).astype(BF)
        low_far = swap(low, 2)
        own, away = jnp.concatenate([near_back, low], 0), jnp.concatenate([far_back, low_far], 0)
        if turn:
            own, away = own.T, away.T
        return own, swap(own, 1), away, swap(away, 1)

    both = jnp.concatenate([inputs, upstream], 0)
    near, far, back = contract(both)
    back_and_query = mp_order(*project(near, far, back, query_slab, output_slab, False), y_lo, core)
    grown_both = expand(jnp.concatenate([back_and_query[tokens:], back_and_query[:tokens]], 0))
    early = back_and_query.T
    early = with_layout_constraint(early, Layout((0, 1)))
    near, far, back = contract(grown_both)
    near, early = lax.optimization_barrier((near, early))
    late = project(near, far, back, output_slab, query_slab, True)

    scale = 1.0 / math.sqrt(tokens * X * Z * Y)
    first_width = features * 3 // 8
    last_width = features - first_width
    part = Z * Y * rows
    ordered, *second = call_product(
        functools.partial(last_kernel, scale, last_width),
        jnp.stack([z, mp]),
        (*late, early.reshape(X, Z, Y * rows, -1), both, grown_both),
        [(X, Z, Y * rows, 2 * tokens)] + [(X, Y * rows, last_width)] * Z,
        3e-6,
    )
    first = call_product(
        functools.partial(first_kernel, scale, first_width),
        x.reshape(1),
        (ordered.reshape(X, part, -1), early.reshape(X, part, -1), both, grown_both),
        [(part, first_width)] * X,
        3e-6,
    )
    grown = dot(ordered.reshape(X * part, -1)[:, tokens:], operator, ((0,), (0,))).astype(BF)
    return scatter_gradient(first, second, grown, x, z, y)


def solution(mesh):
    return jax.shard_map(
        on_device,
        mesh=mesh,
        in_specs=(P("dp", "mp"), P("dp", "mp"), P("dp", "mp"), P("dp", "mp"), P("dp", "mp")),
        out_specs=(P("dp", "mp"), P("dp", "mp")),
        check_vma=False,
    )
```
